256 devices in a mesh: dom: 64 (over z_hi, x, y), inner: 4 (over z_lo, core).
Axes of the slice: x: 4, y: 4, z: 8 (z_hi: 4, z_lo: 2; z = z_hi * 2 + z_lo), core: 2. Of those that a mesh axis runs over, the one named last changes fastest.
Arguments:
- features: bfloat16 [32768, 128], P(('dom', 'inner')), may hold values from -200 to 200
- adjacency: bfloat16 [32768, 32768], P(('dom', 'inner')), may hold values from 0 to 3, as said below
- tile_mask: int32 [256, 64], P(('dom', 'inner')), may hold values 0 or 1
- skip_owner: int32 [64], replicated, may hold values 0 or 1
- weight: bfloat16 [128, 256], replicated, may hold values from -0.5 to 0.5
- bias: float32 [256], replicated, may hold values from -3 to 3
- cotangent: bfloat16 [32768, 256], P(('dom', 'inner')), may hold values from -6 to 6
Outputs:
- activated: bfloat16 [32768, 256], P(('dom', 'inner'))
- grad_weight: float32 [128, 256], replicated
- grad_bias: float32 [256], replicated
The draws below stay inside these ranges and needn't reach their ends.
Inputs may be any that keep to these rules, and one draw needn't show every extreme that they name: `adjacency`: edge weights are 0 or between 0.1 and 3; each row has some 32 nonzero entries on average, spread over all partitions.
All inputs are finite; a program needn't handle non-finite values. Where the reference program divides by a largest or mean magnitude, that divisor is 1e-20 or more. No bound on the sum of `tile_mask` on one device may be relied on, other than what follows from the above.
Results may differ from the reference program's by a relative error of at most 0.0064.
Values may be sent and summed in bfloat16 or wider, within the bound.
No kernel may reach another device: no remote copies, remote signals or barrier semaphores. Data moves between devices by JAX's collectives and lax.ppermute only.
A program may use at most 64 MiB of HBM per device.

```python
import math
import jax
import jax.numpy as jnp
from jax import lax

F_IN = 128
HID = 256
NODE_DEV = 128
P_NODES = 512
NODES = 32768
N_DOM = 64
DEVICES = 256


def draw_features(key, part):
    key = jax.random.fold_in(key, 2)
    first, second = jax.random.split(key, 2)
    base = jax.random.normal(first, (NODES, F_IN), jnp.float32)
    base = jnp.clip(base, -4.0, 4.0)
    spread = jnp.exp(jax.random.uniform(second, (NODES, 1), jnp.float32, 0.0, math.log(10.0)))
    rising = jnp.exp(math.log(3.0) * jnp.arange(NODES, dtype=jnp.float32) / NODES)[:, None]
    return (base * spread * rising).astype(jnp.bfloat16)


def draw_adjacency(key, part):
    key = jax.random.fold_in(key, 1)
    first, second = jax.random.split(key)
    values = jax.random.uniform(first, (NODES, NODES), jnp.float32, 0.5, 2.0)
    links = jax.random.randint(second, (NODES, NODES), 0, NODES // 32) == 0
    return jnp.where(links, values, 0.0).astype(jnp.bfloat16)


def set_ends(array, key, smallest, largest):
    longest = array.shape.index(max(array.shape))
    spots = []
    for shift in (0, 1):
        where = [jax.random.randint(jax.random.fold_in(key, axis), (), 0, length) for axis, length in enumerate(array.shape)]
        where[longest] = (where[longest] + shift) % array.shape[longest]
        spots.append(tuple(where))
    return array.at[spots[0]].set(smallest).at[spots[1]].set(largest)


def shard_levels(rng, shape, cuts, low, high):
    factor_of, own = 1.0, jax.random.fold_in(rng, 6)
    for dim, parts in cuts:
        draws = jnp.exp(jax.random.uniform(jax.random.fold_in(own, dim), (parts,), jnp.float32, low / len(cuts), high / len(cuts)))
        factor_of = factor_of * jnp.repeat(draws, shape[dim] // parts).reshape([-1 if axis == dim else 1 for axis in range(len(shape))])
    return factor_of


def bell_draw(rng, shape, width, limit, shards=(), kind=jnp.bfloat16):
    level = shard_levels(rng, shape, shards, -0.22, 0.18) if shards else 1.0
    values = jax.random.normal(rng, shape, jnp.float32) * width * level
    return jnp.minimum(jnp.maximum(values, -limit), limit).astype(kind)


def setup_inputs(seed: int = 0) -> dict:
    key_list = jax.random.split(jax.random.key(seed), 8)
    return {
        "features": draw_features(jax.random.fold_in(key_list[7], 71), 0),
        "adjacency": draw_adjacency(jax.random.fold_in(key_list[7], 71), 0),
        "tile_mask": set_ends((jax.random.randint(key_list[2], (DEVICES, N_DOM), 0, 4) < 3).astype(jnp.int32), jax.random.fold_in(key_list[2], 1), 0, 1),
        "skip_owner": set_ends((jax.random.randint(key_list[3], (N_DOM,), 0, 4) < 1).astype(jnp.int32), jax.random.fold_in(key_list[3], 1), 0, 1),
        "weight": bell_draw(key_list[4], (F_IN, HID), F_IN ** -0.5, 0.5),
        "bias": bell_draw(key_list[5], (HID,), 0.5, 3.0, (), jnp.float32),
        "cotangent": bell_draw(key_list[6], (NODES, HID), 1.0, 6.0, ((0, 256),)),
    }


def silu_slope(values):
    sigma = jax.nn.sigmoid(values)
    return sigma * (1.0 + values * (1.0 - sigma))


def reference(features, adjacency, tile_mask, skip_owner, weight, bias, cotangent):
    wide = features.astype(jnp.float32)
    shared = jnp.max(jnp.abs(wide)) + 1e-6
    scaled = (wide * (64.0 / shared)).astype(jnp.bfloat16)
    live_parts = 1 - skip_owner

    def one_block(device):
        first_row = device * NODE_DEV
        adj_rows = lax.dynamic_slice_in_dim(adjacency, first_row, NODE_DEV, 0)
        self_rows = lax.dynamic_slice_in_dim(scaled, first_row, NODE_DEV, 0)
        live_tiles = tile_mask[device] * live_parts
        live_cols = jnp.repeat(live_tiles, P_NODES).astype(jnp.bfloat16)
        masked = adj_rows * live_cols[None, :]
        summed = jnp.dot(masked, scaled, preferred_element_type=jnp.float32) + self_rows.astype(jnp.float32)
        degree = 1.0 + jnp.sum(masked.astype(jnp.float32), axis=1)
        return (summed / degree[:, None]).astype(jnp.bfloat16)

    mixed = lax.map(one_block, jnp.arange(DEVICES, dtype=jnp.int32)).reshape(NODES, F_IN)
    pre = jnp.dot(mixed, weight, preferred_element_type=jnp.float32) + bias[None, :]
    activated = jax.nn.silu(pre).astype(jnp.bfloat16)
    delta = cotangent.astype(jnp.float32) * silu_slope(pre)
    delta_low = delta.astype(jnp.bfloat16)
    grad_weight = jnp.dot(mixed.T, delta_low, preferred_element_type=jnp.float32)
    grad_bias = jnp.sum(delta, axis=0)
    return activated, grad_weight, grad_bias
```

```python
import jax
import jax.numpy as jnp
from jax import lax
from jax.experimental import pallas as pl
from jax.experimental.pallas import tpu as pltpu
from jax.sharding import Mesh, PartitionSpec as P

NAMES = ("zh", "x", "y", "zl", "core")
SIZES = (4, 4, 4, 2, 2)
XY = ("x", "y")
ZC = ("zh", "zl", "core")
SHIFTS = (0, 1, 3, 2)
PIECES = 8
PIECE = 4096
BLOCKS = PIECE // 128
VMEM_LIMIT = 60 * 1024 * 1024


def index_of(zh, x, y, zl, core):
    return (((zh * 4 + x) * 4 + y) * 2 + zl) * 2 + core


def coords():
    return [
        (zh, x, y, zl, core)
        for zh in range(4)
        for x in range(4)
        for y in range(4)
        for zl in range(2)
        for core in range(2)
    ]


def permute(array, move):
    return lax.ppermute(array, NAMES, [(index_of(*at), index_of(*move(*at))) for at in coords()])


def swap_cores(array):
    return permute(array, lambda zh, x, y, zl, core: (zh, x, y, zl, 1 - core))


def along_z(array, step):
    def move(zh, x, y, zl, core):
        z = zh * 2 + zl
        if core == 0:
            z = (z + step) % 8 if step < 4 else z
        else:
            z = (z - step) % 8
        return z // 2, x, y, z % 2, core

    return permute(array, move)


def along_xy(array, step, turned):
    def move(zh, x, y, zl, core):
        if (core == 0) != turned:
            return zh, (x + step) % 4, y, zl, core
        return zh, x, (y + step) % 4, zl, core

    return permute(array, move)


def block_table():
    zh, x, y, zl, core = (lax.axis_index(n) for n in NAMES)
    z = zh * 2 + zl
    place = lax.iota(jnp.int32, PIECES * BLOCKS)
    piece, within = place >> 5, place & 31

    def shift_of(slot):
        return jnp.where(slot == 2, 3, jnp.where(slot == 3, 2, slot))

    outer, half = shift_of(piece >> 1), piece & 1
    inner, hop, pair = shift_of(within >> 3), (within >> 1) & 3, within & 1
    plane = core ^ half
    first = plane == 0
    at_x = (x - jnp.where(first, inner, outer)) & 3
    at_y = (y - jnp.where(first, outer, inner)) & 3
    at_z = (z + jnp.where(first, -hop, jnp.where(hop == 0, 4, hop))) & 7
    return index_of(at_z >> 1, at_x, at_y, at_z & 1, pair ^ plane)


def order_kernel(table, tile_mask, skip_owner, adjacency, *outs):
    pieces, degree = outs[:PIECES], outs[PIECES]
    total = jnp.zeros((128, 128), jnp.float32)
    for number, out in enumerate(pieces):

        def one_block(block, total, number=number, out=out):
            source = table[number * BLOCKS + block]
            owner = source >> 2
            live = tile_mask[0, owner] * (1 - skip_owner[owner])
            values = adjacency[:, pl.ds(pl.multiple_of(source * 128, 128), 128)]
            values = values * jnp.full((1, 1), live.astype(jnp.float32)).astype(jnp.bfloat16)
            out[:, pl.ds(pl.multiple_of(block * 128, 128), 128)] = values
            return total + values.astype(jnp.float32)

        total = lax.fori_loop(0, BLOCKS, one_block, total)
    degree[...] = jnp.broadcast_to(1.0 + jnp.sum(total, axis=1, keepdims=True), (128, 128))


def order_adjacency(table, tile_mask, skip_owner, adjacency):
    smem = pl.BlockSpec(memory_space=pltpu.SMEM)
    vmem = pl.BlockSpec(memory_space=pltpu.VMEM)
    return pl.pallas_call(
        order_kernel,
        out_shape=[jax.ShapeDtypeStruct((128, PIECE), jnp.bfloat16)] * PIECES
        + [jax.ShapeDtypeStruct((128, 128), jnp.float32)],
        in_specs=[smem, smem, smem, vmem],
        out_specs=[vmem] * (PIECES + 1),
        compiler_params=pltpu.CompilerParams(vmem_limit_bytes=VMEM_LIMIT),
        cost_estimate=pl.CostEstimate(flops=2 * 128 * 32768, bytes_accessed=4 * 128 * 32768, transcendentals=0),
    )(table, tile_mask, skip_owner, adjacency)


def add_piece(adj, feat, total, largest):
    for start in range(0, PIECE, 512):
        rows = feat[start : start + 512, :]
        total = total + jnp.dot(adj[:, start : start + 512], rows, preferred_element_type=jnp.float32)
        largest = jnp.maximum(largest, jnp.max(jnp.abs(rows).reshape(32, 16, 128), axis=0))
    return total, largest


def piece_kernel(adj_a, adj_b, feat_a, feat_b, total_in, largest_in, total_out, largest_out):
    total, largest = add_piece(adj_a, feat_a, total_in[...], largest_in[...])
    total, largest = add_piece(adj_b, feat_b, total, largest)
    total_out[...] = total
    largest_out[...] = largest


def piece_step(adj_a, adj_b, feat_a, feat_b, total, largest):
    vmem = pl.BlockSpec(memory_space=pltpu.VMEM)
    return pl.pallas_call(
        piece_kernel,
        out_shape=[
            jax.ShapeDtypeStruct((128, 128), jnp.float32),
            jax.ShapeDtypeStruct((16, 128), jnp.bfloat16),
        ],
        in_specs=[vmem] * 6,
        out_specs=[vmem] * 2,
        compiler_params=pltpu.CompilerParams(vmem_limit_bytes=VMEM_LIMIT // 4),
        cost_estimate=pl.CostEstimate(
            flops=4 * 128 * PIECE * 128, bytes_accessed=8 * 128 * PIECE, transcendentals=0
        ),
    )(adj_a, adj_b, feat_a, feat_b, total, largest)


def last_kernel(
    adj_a, adj_b, feat_a, feat_b, total_in, largest_in, own, degree, weight, bias, cotangent, activated, grads
):
    total, largest = add_piece(adj_a, feat_a, total_in[...], largest_in[...])
    total, largest = add_piece(adj_b, feat_b, total, largest)
    factor = 64.0 / (jnp.max(largest.astype(jnp.float32)) + 1e-06)
    summed = (total + own[...].astype(jnp.float32)) * factor
    mixed = (summed / degree[...]).astype(jnp.bfloat16)
    pre = jnp.dot(mixed, weight[...], preferred_element_type=jnp.float32) + bias[...]
    sigma = jax.nn.sigmoid(pre)
    activated[...] = (pre * sigma).astype(jnp.bfloat16)
    delta = cotangent[...].astype(jnp.float32) * (sigma * (1.0 + pre * (1.0 - sigma)))
    grad_weight = lax.dot_general(
        mixed, delta.astype(jnp.bfloat16), (((0,), (0,)), ((), ())), preferred_element_type=jnp.float32
    )
    grad_bias = jnp.sum(delta, axis=0, keepdims=True)
    grads[:, :, :256] = grad_weight.reshape(16, 8, 256)
    row = lax.broadcasted_iota(jnp.int32, (8, 128), 0)
    side = jnp.where(row == 0, grad_bias[:, :128], jnp.where(row == 1, grad_bias[:, 128:], 0.0))
    grads[:, :, 256:] = jnp.broadcast_to(side[None], (16, 8, 128))


def last_step(*args):
    vmem = pl.BlockSpec(memory_space=pltpu.VMEM)
    return pl.pallas_call(
        last_kernel,
        out_shape=[
            jax.ShapeDtypeStruct((128, 256), jnp.bfloat16),
            jax.ShapeDtypeStruct((16, 8, 384), jnp.float32),
        ],
        in_specs=[vmem] * 11,
        out_specs=[vmem] * 2,
        compiler_params=pltpu.CompilerParams(vmem_limit_bytes=VMEM_LIMIT // 4),
        cost_estimate=pl.CostEstimate(
            flops=4 * 128 * PIECE * 128, bytes_accessed=8 * 128 * PIECE, transcendentals=32768
        ),
    )(*args)


def sum_kernel(parts, out):
    out[...] = jnp.broadcast_to(jnp.sum(parts[...], axis=0)[None], out.shape)


def sum_last_kernel(parts, weight_out, bias_out):
    total = jnp.sum(parts[...], axis=0)
    weight_out[...] = jnp.broadcast_to(total[None, :, :256], weight_out.shape)
    bias_out[:, :128] = total[0:1, 256:]
    bias_out[:, 128:] = total[1:2, 256:]


def sum_over_devices(grads):
    part = lax.all_to_all(grads, XY, 0, 0, tiled=True)
    part = pl.pallas_call(sum_kernel, out_shape=jax.ShapeDtypeStruct((16, 8, 384), jnp.float32))(part)
    part = lax.all_to_all(part, ZC, 0, 0, tiled=True)
    part, grad_bias = pl.pallas_call(
        sum_last_kernel,
        out_shape=[
            jax.ShapeDtypeStruct((16, 8, 256), jnp.float32),
            jax.ShapeDtypeStruct((1, 256), jnp.float32),
        ],
    )(part)
    grad_weight = lax.all_to_all(part, XY, 0, 0, tiled=True).reshape(128, 256)
    return grad_weight, grad_bias.reshape(256)


def local(features, adjacency, tile_mask, skip_owner, weight, bias, cotangent):
    ordered = order_adjacency(block_table(), tile_mask, skip_owner, adjacency)
    adj, degree = ordered[:PIECES], ordered[PIECES]
    chip = jnp.concatenate([features, swap_cores(features)])
    far = along_z(chip, 4)
    line = jnp.concatenate([far] + [along_z(chip, step) for step in (3, 2, 1)][::-1])
    plane = jnp.concatenate([line] + [along_xy(line, step, False) for step in SHIFTS[1:]])
    mine = [plane] + [along_xy(plane, step, True) for step in SHIFTS[1:]]
    total = jnp.zeros((128, 128), jnp.float32)
    largest = jnp.zeros((16, 128), jnp.bfloat16)
    for number in range(3):
        feats = mine[number], swap_cores(mine[number])
        total, largest = piece_step(*adj[2 * number : 2 * number + 2], *feats, total, largest)
    activated, grads = last_step(
        *adj[6:8], mine[3], swap_cores(mine[3]), total, largest,
        features, degree, weight, bias.reshape(1, 256), cotangent,
    )
    return (activated, *sum_over_devices(grads))


def solution(mesh):
    fine = Mesh(mesh.devices.reshape(SIZES), NAMES)
    rows = P(NAMES, None)
    return jax.shard_map(
        local,
        mesh=fine,
        in_specs=(rows, rows, rows, P(), P(), P(), rows),
        out_specs=(rows, P(), P()),
        check_vma=False,
    )
```

```python
import functools

import jax
import jax.numpy as jnp
from jax import lax
from jax.experimental import pallas as pl
from jax.experimental.pallas import tpu as pltpu
from jax.sharding import Mesh, PartitionSpec as P

NAMES = ("zh", "x", "y", "zl", "core")
SIZES = (4, 4, 4, 2, 2)
SHIFTS = (0, 1, 3, 2)
PIECES = 8
PIECE = 4096
HALF = PIECE // 2
BLOCKS = PIECE // 128
VMEM_LIMIT = 24 * 1024 * 1024


def index_of(zh, x, y, zl, core):
    return (((zh * 4 + x) * 4 + y) * 2 + zl) * 2 + core


def coords():
    return [
        (zh, x, y, zl, core)
        for zh in range(4)
        for x in range(4)
        for y in range(4)
        for zl in range(2)
        for core in range(2)
    ]


def permute(array, move):
    return lax.ppermute(array, NAMES, [(index_of(*at), index_of(*move(*at))) for at in coords()])


def swap_cores(array):
    return permute(array, lambda zh, x, y, zl, core: (zh, x, y, zl, 1 - core))


def along_z(array, step):
    def move(zh, x, y, zl, core):
        z = zh * 2 + zl
        if core == 0:
            z = (z + step) % 8 if step < 4 else z
        else:
            z = (z - step) % 8
        return z // 2, x, y, z % 2, core

    return permute(array, move)


def swap_pairs(array):
    return permute(array, lambda zh, x, y, zl, core: (zh, x, y, 1 - zl, core))


def along_zh(array, step):
    return permute(array, lambda zh, x, y, zl, core: ((zh + step) % 4, x, y, zl, core))


def along_xy(array, step, turned):
    def move(zh, x, y, zl, core):
        if (core == 0) != turned:
            return zh, (x + step) % 4, y, zl, core
        return zh, x, (y + step) % 4, zl, core

    return permute(array, move)


def place_table(tile_mask, skip_owner):
    zh, x, y, _, core = (lax.axis_index(n) for n in NAMES)
    z = zh * 2 + lax.axis_index("zl")
    source = lax.iota(jnp.int32, PIECES * BLOCKS)
    up = (z - ((source >> 6) * 2 + ((source >> 1) & 1))) & 7
    first = up < 4
    plane = jnp.where(first, 0, 1)

    def slot_of(shift):
        return shift ^ (shift >> 1)

    from_x, from_y = slot_of((x - (source >> 4)) & 3), slot_of((y - (source >> 2)) & 3)
    outer, inner = jnp.where(first, from_y, from_x), jnp.where(first, from_x, from_y)
    hop = jnp.where(first, up, (8 - up) & 3)
    pair = (source & 1) ^ plane
    place = outer * 64 + (plane ^ core) * 32 + inner * 8 + hop * 2 + pair
    return jnp.concatenate([place, tile_mask[0] * (1 - skip_owner)])


def order_kernel(table, adjacency, ordered, degree):
    chunk = pl.program_id(0)

    def one_partition(owner, total):
        owner = chunk * (BLOCKS // 4) + owner
        live = table[PIECES * BLOCKS + owner].astype(jnp.float32)
        live = jnp.full((1, 1), live).astype(jnp.bfloat16)
        for block in range(4):
            place = table[owner * 4 + block]
            start = (owner * 4 + block - chunk * BLOCKS) * 128
            values = adjacency[:, pl.ds(pl.multiple_of(start, 128), 128)] * live
            ordered[place >> 5, :, pl.ds(pl.multiple_of((place & 31) * 128, 128), 128)] = values
            total = total + values.astype(jnp.float32)
        return total

    @pl.when(chunk == 0)
    def _():
        degree[...] = jnp.zeros_like(degree)

    degree[...] = lax.fori_loop(0, BLOCKS // 4, one_partition, degree[...], unroll=2)

    @pl.when(chunk == PIECES - 1)
    def _():
        degree[...] = jnp.broadcast_to(1.0 + jnp.sum(degree[...], axis=1, keepdims=True), (128, 128))


def order_adjacency(table, adjacency):
    vmem = pl.BlockSpec(memory_space=pltpu.VMEM)
    return pl.pallas_call(
        order_kernel,
        out_shape=[
            jax.ShapeDtypeStruct((PIECES, 128, PIECE), jnp.bfloat16),
            jax.ShapeDtypeStruct((128, 128), jnp.float32),
        ],
        grid=(PIECES,),
        in_specs=[pl.BlockSpec(memory_space=pltpu.SMEM), pl.BlockSpec((128, PIECE), lambda chunk: (0, chunk))],
        out_specs=[vmem, vmem],
        compiler_params=pltpu.CompilerParams(vmem_limit_bytes=VMEM_LIMIT),
        cost_estimate=pl.CostEstimate(flops=1024, bytes_accessed=1024, transcendentals=0),
    )(table, adjacency)


def add_piece(ordered, piece, feat, total, largest, first=0):
    for start in range(0, feat.shape[0], 512):
        rows = feat[start : start + 512, :]
        columns = ordered[piece, :, first + start : first + start + 512]
        total = total + jnp.dot(columns, rows, preferred_element_type=jnp.float32)
        largest = jnp.maximum(largest, jnp.max(jnp.abs(rows).reshape(32, 16, 128), axis=0))
    return total, largest


def piece_kernel(piece, ordered, feat_a, feat_b, total_in, largest_in, total_out, largest_out):
    total, largest = add_piece(ordered, piece, feat_a, total_in[...], largest_in[...])
    total, largest = add_piece(ordered, piece + 1, feat_b, total, largest)
    total_out[...] = total
    largest_out[...] = largest


def piece_step(piece, ordered, feat_a, feat_b, total, largest):
    vmem = pl.BlockSpec(memory_space=pltpu.VMEM)
    return pl.pallas_call(
        functools.partial(piece_kernel, piece),
        out_shape=[
            jax.ShapeDtypeStruct((128, 128), jnp.float32),
            jax.ShapeDtypeStruct((16, 128), jnp.bfloat16),
        ],
        in_specs=[vmem] * 5,
        out_specs=[vmem] * 2,
        compiler_params=pltpu.CompilerParams(vmem_limit_bytes=VMEM_LIMIT // 2),
        cost_estimate=pl.CostEstimate(flops=1024, bytes_accessed=1024, transcendentals=0),
    )(ordered, feat_a, feat_b, total, largest)


def last_kernel(
    core, ordered, feat_a, feat_a2, feat_b, feat_b2, total_in, largest_in,
    own, degree, weight, bias, cotangent, activated, mine, theirs,
):
    total, largest = total_in[...], largest_in[...]
    for number, feat in enumerate((feat_a, feat_a2, feat_b, feat_b2)):
        total, largest = add_piece(ordered, 6 + number // 2, feat, total, largest, number % 2 * HALF)
    factor = 64.0 / (jnp.max(largest.astype(jnp.float32)) + 1e-06)
    summed = (total + own[...].astype(jnp.float32)) * factor
    mixed = (summed / degree[...]).astype(jnp.bfloat16)
    pre = jnp.dot(mixed, weight[...], preferred_element_type=jnp.float32) + bias[...]
    sigma = jax.nn.sigmoid(pre)
    activated[...] = (pre * sigma).astype(jnp.bfloat16)
    delta = cotangent[...].astype(jnp.float32) * (sigma * (1.0 + pre * (1.0 - sigma)))
    grad_weight = lax.dot_general(
        mixed, delta.astype(jnp.bfloat16), (((0,), (0,)), ((), ())), preferred_element_type=jnp.float32
    )
    grad_bias = jnp.sum(delta, axis=0, keepdims=True)
    for half in range(2):
        columns = slice(half * 128, half * 128 + 128)

        @pl.when(core[0] == half)
        def _(columns=columns):
            mine[:128, :] = grad_weight[:, columns]
            mine[128:, :] = jnp.broadcast_to(grad_bias[:, columns], (8, 128))

        @pl.when(core[0] != half)
        def _(columns=columns):
            theirs[:128, :] = grad_weight[:, columns]
            theirs[128:, :] = jnp.broadcast_to(grad_bias[:, columns], (8, 128))


def last_step(*args):
    vmem = pl.BlockSpec(memory_space=pltpu.VMEM)
    return pl.pallas_call(
        last_kernel,
        out_shape=[
            jax.ShapeDtypeStruct((128, 256), jnp.bfloat16),
            jax.ShapeDtypeStruct((136, 128), jnp.float32),
            jax.ShapeDtypeStruct((136, 128), jnp.float32),
        ],
        in_specs=[pl.BlockSpec(memory_space=pltpu.SMEM)] + [vmem] * 12,
        out_specs=[vmem] * 3,
        compiler_params=pltpu.CompilerParams(vmem_limit_bytes=VMEM_LIMIT // 2),
        cost_estimate=pl.CostEstimate(flops=1024, bytes_accessed=1024, transcendentals=0),
    )(*args)


def ring_sum(send, part):
    near = send(part, 1) + send(part, 3)
    return (part + send(part, 2)) + near


def sum_over_devices(mine, theirs, core):
    part = mine + swap_cores(theirs)
    for turned in (False, True):
        part = ring_sum(lambda array, step: along_xy(array, step, turned), part)
    part = part + swap_pairs(part)
    part = ring_sum(along_zh, part)
    other = swap_cores(part)
    left, right = jnp.where(core == 0, part, other), jnp.where(core == 0, other, part)
    both = jnp.concatenate([left, right], axis=1)
    return both[:128], both[128]


def local(features, adjacency, tile_mask, skip_owner, weight, bias, cotangent):
    ordered, degree = order_adjacency(place_table(tile_mask, skip_owner), adjacency)
    chip = jnp.concatenate([features, swap_cores(features)])
    far = along_z(chip, 4)
    line = jnp.concatenate([far] + [along_z(chip, step) for step in (3, 2, 1)][::-1])
    plane = jnp.concatenate([line] + [along_xy(line, step, False) for step in SHIFTS[1:]])
    after, before = along_xy(plane, 1, True), along_xy(plane, 3, True)
    total = jnp.zeros((128, 128), jnp.float32)
    largest = jnp.zeros((16, 128), jnp.bfloat16)
    total, largest = piece_step(0, ordered, plane, swap_cores(plane), total, largest)
    after, before, total = lax.optimization_barrier((after, before, total))
    halves = along_xy(after[:HALF], 1, True), along_xy(before[HALF:], 3, True)
    for number, feat in ((1, after), (2, before)):
        total, largest = piece_step(2 * number, ordered, feat, swap_cores(feat), total, largest)
    *halves, total = lax.optimization_barrier((*halves, total))
    core = lax.axis_index("core")
    activated, mine, theirs = last_step(
        core.reshape(1), ordered, *halves, *(swap_cores(half) for half in halves), total, largest,
        features, degree, weight, bias.reshape(1, 256), cotangent,
    )
    return (activated, *sum_over_devices(mine, theirs, core))


def solution(mesh):
    fine = Mesh(mesh.devices.reshape(SIZES), NAMES)
    rows = P(NAMES, None)
    return jax.shard_map(
        local,
        mesh=fine,
        in_specs=(rows, rows, rows, P(), P(), P(), rows),
        out_specs=(rows, P(), P()),
        check_vma=False,
    )
```

```python
import functools

import jax
import jax.numpy as jnp
from jax import lax
from jax.experimental import pallas as pl
from jax.experimental.pallas import tpu as pltpu
from jax.sharding import Mesh, PartitionSpec as P

NAMES = ("zh", "x", "y", "zl", "core")
SIZES = (4, 4, 4, 2, 2)
SHIFTS = (0, 1, 3, 2)
PIECES = 8
PIECE = 4096
HALF = PIECE // 2
FIRST = 3
BLOCKS = PIECE // 128
VMEM_LIMIT = 24 * 1024 * 1024


def index_of(zh, x, y, zl, core):
    return (((zh * 4 + x) * 4 + y) * 2 + zl) * 2 + core


def coords():
    return [
        (zh, x, y, zl, core)
        for zh in range(4)
        for x in range(4)
        for y in range(4)
        for zl in range(2)
        for core in range(2)
    ]


def permute(array, move):
    return lax.ppermute(array, NAMES, [(index_of(*at), index_of(*move(*at))) for at in coords()])


def swap_cores(array):
    return permute(array, lambda zh, x, y, zl, core: (zh, x, y, zl, 1 - core))


def along_z(array, step):
    def move(zh, x, y, zl, core):
        z = zh * 2 + zl
        if core == 0:
            z = (z + step) % 8 if step < 4 else z
        else:
            z = (z - step) % 8
        return z // 2, x, y, z % 2, core

    return permute(array, move)


def swap_pairs(array):
    return permute(array, lambda zh, x, y, zl, core: (zh, x, y, 1 - zl, core))


def along_zh(array, step):
    return permute(array, lambda zh, x, y, zl, core: ((zh + step) % 4, x, y, zl, core))


def along_xy(array, step, turned):
    def move(zh, x, y, zl, core):
        if (core == 0) != turned:
            return zh, (x + step) % 4, y, zl, core
        return zh, x, (y + step) % 4, zl, core

    return permute(array, move)


def place_table(tile_mask, skip_owner):
    zh, x, y, _, core = (lax.axis_index(n) for n in NAMES)
    z = zh * 2 + lax.axis_index("zl")
    source = lax.iota(jnp.int32, PIECES * BLOCKS)
    up = (z - ((source >> 6) * 2 + ((source >> 1) & 1))) & 7
    first = up < 4
    plane = jnp.where(first, 0, 1)

    def slot_of(shift):
        return shift ^ (shift >> 1)

    from_x, from_y = slot_of((x - (source >> 4)) & 3), slot_of((y - (source >> 2)) & 3)
    outer, inner = jnp.where(first, from_y, from_x), jnp.where(first, from_x, from_y)
    hop = jnp.where(first, up, (8 - up) & 3)
    pair = (source & 1) ^ plane
    place = (plane ^ core) * 128 + outer * 32 + inner * 8 + hop * 2 + pair
    return jnp.concatenate([place, tile_mask[0] * (1 - skip_owner)])


def order_kernel(first, table, adjacency, *refs):
    own, give, degree = refs[-3:]
    chunk = pl.program_id(0) + first

    if first == 0:

        @pl.when(chunk == 0)
        def _():
            degree[...] = jnp.zeros_like(degree)

    else:

        @pl.when(chunk == first)
        def _():
            degree[...] = refs[2][...]

    def put(out, low):
        total = degree[...]
        for chip in range(low, BLOCKS // 2, 2):
            live = table[PIECES * BLOCKS + chunk * (BLOCKS // 4) + chip // 2].astype(jnp.float32)
            live = jnp.full((1, 1), live).astype(jnp.bfloat16)
            for block in (chip * 2, chip * 2 + 1):
                spot = table[chunk * BLOCKS + block]
                values = adjacency[:, block * 128 : block * 128 + 128] * live
                out[(spot >> 5) & 3, :, pl.ds(pl.multiple_of((spot & 31) * 128, 128), 128)] = values
                total = total + values.astype(jnp.float32)
        degree[...] = total

    for low in range(2):
        place = table[chunk * BLOCKS + low * 2]
        pl.when(place < 128)(functools.partial(put, own, low))
        pl.when(place >= 128)(functools.partial(put, give, low))

    @pl.when(chunk == PIECES - 1)
    def _():
        degree[...] = jnp.broadcast_to(1.0 + jnp.sum(degree[...], axis=1, keepdims=True), (128, 128))


def order_adjacency(first, count, table, adjacency, *before):
    vmem = pl.BlockSpec(memory_space=pltpu.VMEM)
    return pl.pallas_call(
        functools.partial(order_kernel, first),
        out_shape=[
            jax.ShapeDtypeStruct((PIECES // 2, 128, PIECE), jnp.bfloat16),
            jax.ShapeDtypeStruct((PIECES // 2, 128, PIECE), jnp.bfloat16),
            jax.ShapeDtypeStruct((128, 128), jnp.float32),
        ],
        grid=(count,),
        in_specs=[
            pl.BlockSpec(memory_space=pltpu.SMEM),
            pl.BlockSpec((128, PIECE), lambda chunk: (0, chunk + first)),
            *[vmem] * len(before),
        ],
        out_specs=[vmem] * 3,
        input_output_aliases={2 + number: number for number in range(len(before))},
        compiler_params=pltpu.CompilerParams(vmem_limit_bytes=VMEM_LIMIT),
        cost_estimate=pl.CostEstimate(flops=1024, bytes_accessed=1024, transcendentals=0),
    )(table, pltpu.with_memory_space_constraint(adjacency, pltpu.HBM), *before)


def piece_kernel(spots, last, own, got, *refs):
    feats, (ours, theirs, largest, ours_out, theirs_out, largest_out) = refs[: len(spots)], refs[len(spots) :]
    ours, theirs, largest = ours[...], theirs[...], largest[...]
    for (piece, first), feat in zip(spots, feats, strict=True):
        for start in range(0, feat.shape[0], 512):
            rows = feat[start : start + 512, :]
            columns = slice(first + start, first + start + 512)
            ours = ours + jnp.dot(own[piece, :, columns], rows, preferred_element_type=jnp.float32)
            theirs = theirs + jnp.dot(got[piece, :, columns], rows, preferred_element_type=jnp.float32)
            largest = jnp.maximum(largest, jnp.max(jnp.abs(rows).reshape(32, 16, 128), axis=0))
    ours_out[...] = ours
    largest_out[...] = largest
    theirs_out[:128, :] = theirs
    if last:
        wide = largest.astype(jnp.float32)
        theirs_out[128:, :] = jnp.maximum(wide[:8], wide[8:])


def piece_step(spots, last, own, got, feats, sums):
    vmem = pl.BlockSpec(memory_space=pltpu.VMEM)
    return pl.pallas_call(
        functools.partial(piece_kernel, spots, last),
        out_shape=[
            jax.ShapeDtypeStruct((128, 128), jnp.float32),
            jax.ShapeDtypeStruct((136 if last else 128, 128), jnp.float32),
            jax.ShapeDtypeStruct((16, 128), jnp.bfloat16),
        ],
        in_specs=[vmem] * (5 + len(spots)),
        out_specs=[vmem] * 3,
        compiler_params=pltpu.CompilerParams(vmem_limit_bytes=VMEM_LIMIT // 2),
        cost_estimate=pl.CostEstimate(flops=1024, bytes_accessed=1024, transcendentals=0),
    )(own, got, *feats, *sums)


def last_kernel(
    core, ours, partial, largest_in, own, degree, weight, bias, cotangent, activated, mine, theirs
):
    total = ours[...] + partial[:128, :]
    largest = jnp.maximum(jnp.max(largest_in[...].astype(jnp.float32)), jnp.max(partial[128:, :]))
    factor = 64.0 / (largest + 1e-06)
    summed = (total + own[...].astype(jnp.float32)) * factor
    mixed = (summed / degree[...]).astype(jnp.bfloat16)
    pre = jnp.dot(mixed, weight[...], preferred_element_type=jnp.float32) + bias[...]
    sigma = jax.nn.sigmoid(pre)
    activated[...] = (pre * sigma).astype(jnp.bfloat16)
    delta = cotangent[...].astype(jnp.float32) * (sigma * (1.0 + pre * (1.0 - sigma)))
    grad_weight = lax.dot_general(
        mixed, delta.astype(jnp.bfloat16), (((0,), (0,)), ((), ())), preferred_element_type=jnp.float32
    )
    grad_bias = jnp.sum(delta, axis=0, keepdims=True)
    for half in range(2):
        columns = slice(half * 128, half * 128 + 128)

        @pl.when(core[0] == half)
        def _(columns=columns):
            mine[:128, :] = grad_weight[:, columns]
            mine[128:, :] = jnp.broadcast_to(grad_bias[:, columns], (8, 128))

        @pl.when(core[0] != half)
        def _(columns=columns):
            theirs[:128, :] = grad_weight[:, columns]
            theirs[128:, :] = jnp.broadcast_to(grad_bias[:, columns], (8, 128))


def last_step(*args):
    vmem = pl.BlockSpec(memory_space=pltpu.VMEM)
    return pl.pallas_call(
        last_kernel,
        out_shape=[
            jax.ShapeDtypeStruct((128, 256), jnp.bfloat16),
            jax.ShapeDtypeStruct((136, 128), jnp.float32),
            jax.ShapeDtypeStruct((136, 128), jnp.float32),
        ],
        in_specs=[pl.BlockSpec(memory_space=pltpu.SMEM)] + [vmem] * 8,
        out_specs=[vmem] * 3,
        compiler_params=pltpu.CompilerParams(vmem_limit_bytes=VMEM_LIMIT // 2),
        cost_estimate=pl.CostEstimate(flops=1024, bytes_accessed=1024, transcendentals=0),
    )(*args)


def ring_sum(send, part):
    near = send(part, 1) + send(part, 3)
    return (part + send(part, 2)) + near


def sum_over_devices(mine, theirs, core):
    part = mine + swap_cores(theirs)
    for turned in (False, True):
        part = ring_sum(lambda array, step: along_xy(array, step, turned), part)
    part = part + swap_pairs(part)
    part = ring_sum(along_zh, part)
    other = swap_cores(part)
    left, right = jnp.where(core == 0, part, other), jnp.where(core == 0, other, part)
    both = jnp.concatenate([left, right], axis=1)
    return both[:128], both[128]


def local(features, adjacency, tile_mask, skip_owner, weight, bias, cotangent):
    table = place_table(tile_mask, skip_owner)
    ordered = order_adjacency(0, FIRST, table, adjacency)
    chip = jnp.concatenate([features, swap_cores(features)])
    far = along_z(chip, 4)
    line = jnp.concatenate([far] + [along_z(chip, step) for step in (3, 2, 1)][::-1])
    line, *ordered = lax.optimization_barrier((line, *ordered))
    own, give, degree = order_adjacency(FIRST, PIECES - FIRST, table, adjacency, *ordered)
    plane = jnp.concatenate([line] + [along_xy(line, step, False) for step in SHIFTS[1:]])
    plane, own, give, degree = lax.optimization_barrier((plane, own, give, degree))
    got = swap_cores(give)
    front, back = plane[:HALF], plane[HALF:]
    front_after, back_before = along_xy(front, 1, True), along_xy(back, 3, True)
    back_after, front_before = along_xy(back, 1, True), along_xy(front, 3, True)
    front_after, back_before, got = lax.optimization_barrier((front_after, back_before, got))
    halves = along_xy(front_after, 1, True), along_xy(back_before, 3, True)
    zero = jnp.zeros((128, 128), jnp.float32)
    sums = zero, zero, jnp.zeros((16, 128), jnp.bfloat16)
    sums = piece_step(
        ((0, 0), (1, 0), (2, HALF)), False, own, got, (plane, front_after, back_before), sums
    )
    sums = piece_step(((1, HALF), (2, 0)), False, own, got, (back_after, front_before), sums)
    ours, theirs, largest = piece_step(((3, 0), (3, HALF)), True, own, got, halves, sums)
    core = lax.axis_index("core")
    activated, mine, theirs = last_step(
        core.reshape(1), ours, swap_cores(theirs), largest,
        features, degree, weight, bias.reshape(1, 256), cotangent,
    )
    return (activated, *sum_over_devices(mine, theirs, core))


def solution(mesh):
    fine = Mesh(mesh.devices.reshape(SIZES), NAMES)
    rows = P(NAMES, None)
    return jax.shard_map(
        local,
        mesh=fine,
        in_specs=(rows, rows, rows, P(), P(), P(), rows),
        out_specs=(rows, P(), P()),
        check_vma=False,
    )
```

```python
import functools

import jax
import jax.numpy as jnp
from jax import lax
from jax.experimental import pallas as pl
from jax.experimental.pallas import tpu as pltpu
from jax.sharding import Mesh, PartitionSpec as P

NAMES = ("zh", "x", "y", "zl", "core")
SIZES = (4, 4, 4, 2, 2)
SHIFTS = (0, 1, 3, 2)
PIECES = 8
PIECE = 4096
HALF = PIECE // 2
FIRST = 3
BLOCKS = PIECE // 128
VMEM_LIMIT = 24 * 1024 * 1024


def index_of(zh, x, y, zl, core):
    return (((zh * 4 + x) * 4 + y) * 2 + zl) * 2 + core


def coords():
    return [
        (zh, x, y, zl, core)
        for zh in range(4)
        for x in range(4)
        for y in range(4)
        for zl in range(2)
        for core in range(2)
    ]


def permute(array, move):
    return lax.ppermute(array, NAMES, [(index_of(*at), index_of(*move(*at))) for at in coords()])


def swap_cores(array):
    return permute(array, lambda zh, x, y, zl, core: (zh, x, y, zl, 1 - core))


def along_z(array, step):
    def move(zh, x, y, zl, core):
        z = zh * 2 + zl
        if core == 0:
            z = (z + step) % 8 if step < 4 else z
        else:
            z = (z - step) % 8
        return z // 2, x, y, z % 2, core

    return permute(array, move)


def swap_pairs(array):
    return permute(array, lambda zh, x, y, zl, core: (zh, x, y, 1 - zl, core))


def along_zh(array, step):
    return permute(array, lambda zh, x, y, zl, core: ((zh + step) % 4, x, y, zl, core))


def along_xy(array, step, turned):
    def move(zh, x, y, zl, core):
        if (core == 0) != turned:
            return zh, (x + step) % 4, y, zl, core
        return zh, x, (y + step) % 4, zl, core

    return permute(array, move)


def place_table(tile_mask, skip_owner):
    zh, x, y, _, core = (lax.axis_index(n) for n in NAMES)
    z = zh * 2 + lax.axis_index("zl")
    source = lax.iota(jnp.int32, PIECES * BLOCKS)
    up = (z - ((source >> 6) * 2 + ((source >> 1) & 1))) & 7
    first = up < 4
    plane = jnp.where(first, 0, 1)

    def slot_of(shift):
        return shift ^ (shift >> 1)

    from_x, from_y = slot_of((x - (source >> 4)) & 3), slot_of((y - (source >> 2)) & 3)
    outer, inner = jnp.where(first, from_y, from_x), jnp.where(first, from_x, from_y)
    hop = (3 - jnp.where(first, up, 8 - up)) & 3
    pair = (source & 1) ^ plane
    place = (plane ^ core) * 128 + outer * 32 + inner * 8 + hop * 2 + pair
    return jnp.concatenate([place, tile_mask[0] * (1 - skip_owner)])


def order_kernel(first, table, adjacency, *refs):
    own, give, degree = refs[-3:]
    chunk = pl.program_id(0) + first

    if first == 0:

        @pl.when(chunk == 0)
        def _():
            degree[...] = jnp.zeros_like(degree)

    else:

        @pl.when(chunk == first)
        def _():
            degree[...] = refs[2][...]

    def put(out, low):
        total = degree[...]
        for chip in range(low, BLOCKS // 2, 2):
            live = table[PIECES * BLOCKS + chunk * (BLOCKS // 4) + chip // 2].astype(jnp.float32)
            live = jnp.full((1, 1), live).astype(jnp.bfloat16)
            for block in (chip * 2, chip * 2 + 1):
                spot = table[chunk * BLOCKS + block]
                values = adjacency[:, block * 128 : block * 128 + 128] * live
                out[(spot >> 5) & 3, :, pl.ds(pl.multiple_of((spot & 31) * 128, 128), 128)] = values
                total = total + values.astype(jnp.float32)
        degree[...] = total

    for low in range(2):
        place = table[chunk * BLOCKS + low * 2]
        pl.when(place < 128)(functools.partial(put, own, low))
        pl.when(place >= 128)(functools.partial(put, give, low))

    @pl.when(chunk == PIECES - 1)
    def _():
        degree[...] = jnp.broadcast_to(1.0 + jnp.sum(degree[...], axis=1, keepdims=True), (128, 128))


def order_adjacency(first, count, table, adjacency, *before):
    vmem = pl.BlockSpec(memory_space=pltpu.VMEM)
    return pl.pallas_call(
        functools.partial(order_kernel, first),
        out_shape=[
            jax.ShapeDtypeStruct((PIECES // 2, 128, PIECE), jnp.bfloat16),
            jax.ShapeDtypeStruct((PIECES // 2, 128, PIECE), jnp.bfloat16),
            jax.ShapeDtypeStruct((128, 128), jnp.float32),
        ],
        grid=(count,),
        in_specs=[
            pl.BlockSpec(memory_space=pltpu.SMEM),
            pl.BlockSpec((128, PIECE), lambda chunk: (0, chunk + first)),
            *[vmem] * len(before),
        ],
        out_specs=[vmem] * 3,
        input_output_aliases={2 + number: number for number in range(len(before))},
        compiler_params=pltpu.CompilerParams(vmem_limit_bytes=VMEM_LIMIT),
        cost_estimate=pl.CostEstimate(flops=1024, bytes_accessed=1024, transcendentals=0),
    )(table, pltpu.with_memory_space_constraint(adjacency, pltpu.HBM), *before)


def piece_kernel(spots, last, own, got, *refs):
    feats, (ours, theirs, largest, ours_out, theirs_out, largest_out) = refs[: len(spots)], refs[len(spots) :]
    ours, theirs, largest = ours[...], theirs[...], largest[...]
    for (piece, first), feat in zip(spots, feats, strict=True):
        for start in range(0, feat.shape[0], 512):
            rows = feat[start : start + 512, :]
            columns = slice(first + start, first + start + 512)
            ours = ours + jnp.dot(own[piece, :, columns], rows, preferred_element_type=jnp.float32)
            theirs = theirs + jnp.dot(got[piece, :, columns], rows, preferred_element_type=jnp.float32)
            largest = jnp.maximum(largest, jnp.max(jnp.abs(rows).reshape(32, 16, 128), axis=0))
    ours_out[...] = ours
    largest_out[...] = largest
    theirs_out[:128, :] = theirs
    if last:
        wide = largest.astype(jnp.float32)
        theirs_out[128:, :] = jnp.maximum(wide[:8], wide[8:])


def piece_step(spots, last, own, got, feats, sums):
    vmem = pl.BlockSpec(memory_space=pltpu.VMEM)
    return pl.pallas_call(
        functools.partial(piece_kernel, spots, last),
        out_shape=[
            jax.ShapeDtypeStruct((128, 128), jnp.float32),
            jax.ShapeDtypeStruct((136 if last else 128, 128), jnp.float32),
            jax.ShapeDtypeStruct((16, 128), jnp.bfloat16),
        ],
        in_specs=[vmem] * (5 + len(spots)),
        out_specs=[vmem] * 3,
        compiler_params=pltpu.CompilerParams(vmem_limit_bytes=VMEM_LIMIT // 2),
        cost_estimate=pl.CostEstimate(flops=1024, bytes_accessed=1024, transcendentals=0),
    )(own, got, *feats, *sums)


def last_kernel(
    core, ours, partial, largest_in, own, degree, weight, bias, cotangent, activated, mine, theirs
):
    total = ours[...] + partial[:128, :]
    largest = jnp.maximum(jnp.max(largest_in[...].astype(jnp.float32)), jnp.max(partial[128:, :]))
    factor = 64.0 / (largest + 1e-06)
    summed = (total + own[...].astype(jnp.float32)) * factor
    mixed = (summed / degree[...]).astype(jnp.bfloat16)
    pre = jnp.dot(mixed, weight[...], preferred_element_type=jnp.float32) + bias[...]
    sigma = jax.nn.sigmoid(pre)
    activated[...] = (pre * sigma).astype(jnp.bfloat16)
    delta = cotangent[...].astype(jnp.float32) * (sigma * (1.0 + pre * (1.0 - sigma)))
    grad_weight = lax.dot_general(
        mixed, delta.astype(jnp.bfloat16), (((0,), (0,)), ((), ())), preferred_element_type=jnp.float32
    )
    grad_bias = jnp.sum(delta, axis=0, keepdims=True)
    for half in range(2):
        columns = slice(half * 128, half * 128 + 128)

        @pl.when(core[0] == half)
        def _(columns=columns):
            mine[:128, :] = grad_weight[:, columns]
            mine[128:, :] = jnp.broadcast_to(grad_bias[:, columns], (8, 128))

        @pl.when(core[0] != half)
        def _(columns=columns):
            theirs[:128, :] = grad_weight[:, columns]
            theirs[128:, :] = jnp.broadcast_to(grad_bias[:, columns], (8, 128))


def last_step(*args):
    vmem = pl.BlockSpec(memory_space=pltpu.VMEM)
    return pl.pallas_call(
        last_kernel,
        out_shape=[
            jax.ShapeDtypeStruct((128, 256), jnp.bfloat16),
            jax.ShapeDtypeStruct((136, 128), jnp.float32),
            jax.ShapeDtypeStruct((136, 128), jnp.float32),
        ],
        in_specs=[pl.BlockSpec(memory_space=pltpu.SMEM)] + [vmem] * 8,
        out_specs=[vmem] * 3,
        compiler_params=pltpu.CompilerParams(vmem_limit_bytes=VMEM_LIMIT // 2),
        cost_estimate=pl.CostEstimate(flops=1024, bytes_accessed=1024, transcendentals=0),
    )(*args)


def ring_sum(send, part):
    near = send(part, 1) + send(part, 3)
    return (part + send(part, 2)) + near


def sum_over_devices(mine, theirs, core):
    part = mine + swap_cores(theirs)
    for turned in (False, True):
        part = ring_sum(lambda array, step: along_xy(array, step, turned), part)
    part = part + swap_pairs(part)
    part = ring_sum(along_zh, part)
    other = swap_cores(part)
    left, right = jnp.where(core == 0, part, other), jnp.where(core == 0, other, part)
    both = jnp.concatenate([left, right], axis=1)
    return both[:128], both[128]


def local(features, adjacency, tile_mask, skip_owner, weight, bias, cotangent):
    table = place_table(tile_mask, skip_owner)
    ordered = order_adjacency(0, FIRST, table, adjacency)
    chip = jnp.concatenate([features, swap_cores(features)])
    line = jnp.concatenate([along_z(chip, step) for step in (3, 2, 1, 4)])
    line, *ordered = lax.optimization_barrier((line, *ordered))
    own, give, degree = order_adjacency(FIRST, PIECES - FIRST, table, adjacency, *ordered)
    slots = [line] + [along_xy(line, step, False) for step in SHIFTS[1:]]
    front, back = jnp.concatenate(slots[:2]), jnp.concatenate(slots[2:])
    front, back, own, give, degree = lax.optimization_barrier((front, back, own, give, degree))
    got = swap_cores(give)
    front_after, back_before = along_xy(front, 1, True), along_xy(back, 3, True)
    back_after, front_before = along_xy(back, 1, True), along_xy(front, 3, True)
    front_after, back_before, got = lax.optimization_barrier((front_after, back_before, got))
    halves = along_xy(front_after, 1, True), along_xy(back_before, 3, True)
    zero = jnp.zeros((128, 128), jnp.float32)
    sums = zero, zero, jnp.zeros((16, 128), jnp.bfloat16)
    sums = piece_step(
        ((0, 0), (0, HALF), (1, 0), (2, HALF)), False, own, got, (front, back, front_after, back_before), sums
    )
    sums = piece_step(((1, HALF), (2, 0)), False, own, got, (back_after, front_before), sums)
    ours, theirs, largest = piece_step(((3, 0), (3, HALF)), True, own, got, halves, sums)
    core = lax.axis_index("core")
    activated, mine, theirs = last_step(
        core.reshape(1), ours, swap_cores(theirs), largest,
        features, degree, weight, bias.reshape(1, 256), cotangent,
    )
    return (activated, *sum_over_devices(mine, theirs, core))


def solution(mesh):
    fine = Mesh(mesh.devices.reshape(SIZES), NAMES)
    rows = P(NAMES, None)
    return jax.shard_map(
        local,
        mesh=fine,
        in_specs=(rows, rows, rows, P(), P(), P(), rows),
        out_specs=(rows, P(), P()),
        check_vma=False,
    )
```

```python
import functools

import jax
import jax.numpy as jnp
from jax import lax
from jax.experimental import pallas as pl
from jax.experimental.pallas import tpu as pltpu
from jax.sharding import Mesh, PartitionSpec as P

NAMES = ("zh", "x", "y", "zl", "core")
SIZES = (4, 4, 4, 2, 2)
SHIFTS = (0, 1, 3, 2)
PIECES = 8
PIECE = 4096
HALF = PIECE // 2
FIRST = 3
BLOCKS = PIECE // 128
VMEM_LIMIT = 24 * 1024 * 1024


def index_of(zh, x, y, zl, core):
    return (((zh * 4 + x) * 4 + y) * 2 + zl) * 2 + core


def coords():
    return [
        (zh, x, y, zl, core)
        for zh in range(4)
        for x in range(4)
        for y in range(4)
        for zl in range(2)
        for core in range(2)
    ]


def permute(array, move):
    return lax.ppermute(array, NAMES, [(index_of(*at), index_of(*move(*at))) for at in coords()])


def swap_cores(array):
    return permute(array, lambda zh, x, y, zl, core: (zh, x, y, zl, 1 - core))


def along_z(array, step):
    def move(zh, x, y, zl, core):
        z = zh * 2 + zl
        if core == 0:
            z = (z + step) % 8 if step < 4 else z
        else:
            z = (z - step) % 8
        return z // 2, x, y, z % 2, core

    return permute(array, move)


def swap_pairs(array):
    return permute(array, lambda zh, x, y, zl, core: (zh, x, y, 1 - zl, core))


def along_zh(array, step):
    return permute(array, lambda zh, x, y, zl, core: ((zh + step) % 4, x, y, zl, core))


def along_xy(array, step, turned):
    def move(zh, x, y, zl, core):
        if (core == 0) != turned:
            return zh, (x + step) % 4, y, zl, core
        return zh, x, (y + step) % 4, zl, core

    return permute(array, move)


def place_table(tile_mask, skip_owner):
    zh, x, y, _, core = (lax.axis_index(n) for n in NAMES)
    z = zh * 2 + lax.axis_index("zl")
    source = lax.iota(jnp.int32, PIECES * BLOCKS)
    up = (z - ((source >> 6) * 2 + ((source >> 1) & 1))) & 7
    first = up < 4
    plane = jnp.where(first, 0, 1)

    def slot_of(shift):
        return shift ^ (shift >> 1)

    from_x, from_y = slot_of((x - (source >> 4)) & 3), slot_of((y - (source >> 2)) & 3)
    outer, inner = jnp.where(first, from_y, from_x), jnp.where(first, from_x, from_y)
    hop = (3 - jnp.where(first, up, 8 - up)) & 3
    pair = (source & 1) ^ plane
    place = (plane ^ core) * 128 + outer * 32 + inner * 8 + hop * 2 + pair
    return jnp.concatenate([place, tile_mask[0] * (1 - skip_owner)])


def order_kernel(first, table, adjacency, *refs):
    own, give, degree = refs[-3:]
    chunk = pl.program_id(0) + first

    if first == 0:

        @pl.when(chunk == 0)
        def _():
            degree[...] = jnp.zeros_like(degree)

    else:

        @pl.when(chunk == first)
        def _():
            degree[...] = refs[2][...]

    def put(out, low):
        total = degree[...]
        for chip in range(low, BLOCKS // 2, 2):
            live = table[PIECES * BLOCKS + chunk * (BLOCKS // 4) + chip // 2].astype(jnp.float32)
            live = jnp.full((1, 1), live).astype(jnp.bfloat16)
            for block in (chip * 2, chip * 2 + 1):
                spot = table[chunk * BLOCKS + block]
                values = adjacency[:, block * 128 : block * 128 + 128] * live
                out[(spot >> 5) & 3, :, pl.ds(pl.multiple_of((spot & 31) * 128, 128), 128)] = values
                total = total + values.astype(jnp.float32)
        degree[...] = total

    for low in range(2):
        place = table[chunk * BLOCKS + low * 2]
        pl.when(place < 128)(functools.partial(put, own, low))
        pl.when(place >= 128)(functools.partial(put, give, low))

    @pl.when(chunk == PIECES - 1)
    def _():
        degree[...] = jnp.broadcast_to(1.0 + jnp.sum(degree[...], axis=1, keepdims=True), (128, 128))


def order_adjacency(first, count, table, adjacency, *before):
    vmem = pl.BlockSpec(memory_space=pltpu.VMEM)
    return pl.pallas_call(
        functools.partial(order_kernel, first),
        out_shape=[
            jax.ShapeDtypeStruct((PIECES // 2, 128, PIECE), jnp.bfloat16),
            jax.ShapeDtypeStruct((PIECES // 2, 128, PIECE), jnp.bfloat16),
            jax.ShapeDtypeStruct((128, 128), jnp.float32),
        ],
        grid=(count,),
        in_specs=[
            pl.BlockSpec(memory_space=pltpu.SMEM),
            pl.BlockSpec((128, PIECE), lambda chunk: (0, chunk + first)),
            *[vmem] * len(before),
        ],
        out_specs=[vmem] * 3,
        input_output_aliases={2 + number: number for number in range(len(before))},
        compiler_params=pltpu.CompilerParams(vmem_limit_bytes=VMEM_LIMIT),
        cost_estimate=pl.CostEstimate(flops=1024, bytes_accessed=1024, transcendentals=0),
    )(table, pltpu.with_memory_space_constraint(adjacency, pltpu.HBM), *before)


def piece_kernel(spots, last, own, got, *refs):
    feats, (ours, theirs, largest, ours_out, theirs_out, largest_out) = refs[: len(spots)], refs[len(spots) :]
    ours, theirs, largest = ours[...], theirs[...], largest[...]
    for (piece, first), feat in zip(spots, feats, strict=True):
        for start in range(0, feat.shape[0], 512):
            rows = feat[start : start + 512, :]
            columns = slice(first + start, first + start + 512)
            ours = ours + jnp.dot(own[piece, :, columns], rows, preferred_element_type=jnp.float32)
            theirs = theirs + jnp.dot(got[piece, :, columns], rows, preferred_element_type=jnp.float32)
            largest = jnp.maximum(largest, jnp.max(jnp.abs(rows).reshape(32, 16, 128), axis=0))
    ours_out[...] = ours
    largest_out[...] = largest
    theirs_out[:128, :] = theirs
    if last:
        wide = largest.astype(jnp.float32)
        theirs_out[128:, :] = jnp.maximum(wide[:8], wide[8:])


def piece_step(spots, last, own, got, feats, sums):
    vmem = pl.BlockSpec(memory_space=pltpu.VMEM)
    return pl.pallas_call(
        functools.partial(piece_kernel, spots, last),
        out_shape=[
            jax.ShapeDtypeStruct((128, 128), jnp.float32),
            jax.ShapeDtypeStruct((136 if last else 128, 128), jnp.float32),
            jax.ShapeDtypeStruct((16, 128), jnp.bfloat16),
        ],
        in_specs=[vmem] * (5 + len(spots)),
        out_specs=[vmem] * 3,
        compiler_params=pltpu.CompilerParams(vmem_limit_bytes=VMEM_LIMIT // 2),
        cost_estimate=pl.CostEstimate(flops=1024, bytes_accessed=1024, transcendentals=0),
    )(own, got, *feats, *sums)


def last_kernel(
    core, ours, partial, largest_in, own, degree, weight, bias, cotangent, activated, mine, theirs
):
    total = ours[...] + partial[:128, :]
    largest = jnp.maximum(jnp.max(largest_in[...].astype(jnp.float32)), jnp.max(partial[128:, :]))
    factor = 64.0 / (largest + 1e-06)
    summed = (total + own[...].astype(jnp.float32)) * factor
    mixed = (summed / degree[...]).astype(jnp.bfloat16)
    pre = jnp.dot(mixed, weight[...], preferred_element_type=jnp.float32) + bias[...]
    sigma = jax.nn.sigmoid(pre)
    activated[...] = (pre * sigma).astype(jnp.bfloat16)
    delta = cotangent[...].astype(jnp.float32) * (sigma * (1.0 + pre * (1.0 - sigma)))
    grad_weight = lax.dot_general(
        mixed, delta.astype(jnp.bfloat16), (((0,), (0,)), ((), ())), preferred_element_type=jnp.float32
    )
    grad_bias = jnp.sum(delta, axis=0, keepdims=True)
    for half in range(2):
        columns = slice(half * 128, half * 128 + 128)

        @pl.when(core[0] == half)
        def _(columns=columns):
            mine[:128, :] = grad_weight[:, columns]
            mine[128:, :] = jnp.broadcast_to(grad_bias[:, columns], (8, 128))

        @pl.when(core[0] != half)
        def _(columns=columns):
            theirs[:128, :] = grad_weight[:, columns]
            theirs[128:, :] = jnp.broadcast_to(grad_bias[:, columns], (8, 128))


def last_step(*args):
    vmem = pl.BlockSpec(memory_space=pltpu.VMEM)
    return pl.pallas_call(
        last_kernel,
        out_shape=[
            jax.ShapeDtypeStruct((128, 256), jnp.bfloat16),
            jax.ShapeDtypeStruct((136, 128), jnp.float32),
            jax.ShapeDtypeStruct((136, 128), jnp.float32),
        ],
        in_specs=[pl.BlockSpec(memory_space=pltpu.SMEM)] + [vmem] * 8,
        out_specs=[vmem] * 3,
        compiler_params=pltpu.CompilerParams(vmem_limit_bytes=VMEM_LIMIT // 2),
        cost_estimate=pl.CostEstimate(flops=1024, bytes_accessed=1024, transcendentals=0),
    )(*args)


def ring_sum(send, part):
    near = send(part, 1) + send(part, 3)
    return (part + send(part, 2)) + near


def sum_over_devices(mine, theirs, core):
    part = mine + swap_cores(theirs)
    for turned in (False, True):
        part = ring_sum(lambda array, step: along_xy(array, step, turned), part)
    part = part + swap_pairs(part)
    part = part.astype(jnp.bfloat16).astype(jnp.float32)
    part = ring_sum(lambda array, step: along_zh(array.astype(jnp.bfloat16), step).astype(jnp.float32), part)
    other = swap_cores(part)
    left, right = jnp.where(core == 0, part, other), jnp.where(core == 0, other, part)
    both = jnp.concatenate([left, right], axis=1)
    return both[:128], both[128]


def local(features, adjacency, tile_mask, skip_owner, weight, bias, cotangent):
    table = place_table(tile_mask, skip_owner)
    ordered = order_adjacency(0, FIRST, table, adjacency)
    chip = jnp.concatenate([features, swap_cores(features)])
    line = jnp.concatenate([along_z(chip, step) for step in (3, 2, 1, 4)])
    line, *ordered = lax.optimization_barrier((line, *ordered))
    own, give, degree = order_adjacency(FIRST, PIECES - FIRST, table, adjacency, *ordered)
    slots = [line] + [along_xy(line, step, False) for step in SHIFTS[1:]]
    front, back = jnp.concatenate(slots[:2]), jnp.concatenate(slots[2:])
    front, back, own, give, degree = lax.optimization_barrier((front, back, own, give, degree))
    got = swap_cores(give)
    front_after, back_before = along_xy(front, 1, True), along_xy(back, 3, True)
    back_after, front_before = along_xy(back, 1, True), along_xy(front, 3, True)
    front_after, back_before, got = lax.optimization_barrier((front_after, back_before, got))
    halves = along_xy(front_after, 1, True), along_xy(back_before, 3, True)
    zero = jnp.zeros((128, 128), jnp.float32)
    sums = zero, zero, jnp.zeros((16, 128), jnp.bfloat16)
    sums = piece_step(
        ((0, 0), (0, HALF), (1, 0), (2, HALF)), False, own, got, (front, back, front_after, back_before), sums
    )
    sums = piece_step(((1, HALF), (2, 0)), False, own, got, (back_after, front_before), sums)
    ours, theirs, largest = piece_step(((3, 0), (3, HALF)), True, own, got, halves, sums)
    core = lax.axis_index("core")
    activated, mine, theirs = last_step(
        core.reshape(1), ours, swap_cores(theirs), largest,
        features, degree, weight, bias.reshape(1, 256), cotangent,
    )
    return (activated, *sum_over_devices(mine, theirs, core))


def solution(mesh):
    fine = Mesh(mesh.devices.reshape(SIZES), NAMES)
    rows = P(NAMES, None)
    return jax.shard_map(
        local,
        mesh=fine,
        in_specs=(rows, rows, rows, P(), P(), P(), rows),
        out_specs=(rows, P(), P()),
        check_vma=False,
    )
```
